32 devices in a mesh: groups: 2 (over y), req: 4 (over x, core), tensor: 4 (over z).
Axes of the slice: x: 2, y: 2, z: 4, core: 2. Of those that a mesh axis runs over, the one named last changes fastest.
Arguments:
- hidden: bfloat16 [384, 24576], P(('groups', 'req'), 'tensor'), parts along dimension 0, may hold values from -6 to 6
- join_weight: bfloat16 [24576, 8192], P('tensor', 'req'), may hold values from -0.0390625 to 0.0390625
- norm_gain: bfloat16 [8192], P(('req', 'tensor')), may hold values from 0.099609375 to 1.8984375
- qkv_weight: bfloat16 [8192, 9216], P(('req', 'tensor')), may hold values from -0.0625 to 0.0625
- owner_draft_cache: bfloat16 [48, 512, 2, 512], P(('groups', 'req'), 'tensor'), parts along dimension 0, may hold values from -250 to 250
- node_count: int32 [48], P('groups'), parts along dimension 0, may hold values from 1 to 8, as said below
- owner: int32 [48], P('groups'), parts along dimension 0, may hold values from 0 to 3, as said below
- cache_len: int32 [48], P('groups'), parts along dimension 0, may hold values from 1 to 512, as said below
Outputs:
- draft_attention: bfloat16 [48, 8, 8192], P(('groups', 'req'), None, 'tensor'), parts along dimension 0
The draws below stay inside these ranges and needn't reach their ends.
There are 2 independent parts, one for each index of `groups`. The reference program is written for one: setup_inputs(seed, part) draws one part's arguments, and reference() takes and returns one part's arrays. A program takes and returns all parts, laid end to end along the dimension named above; an argument that names none is the same for every part. Nothing has to cross between parts.
Inputs may be any that keep to these rules, and one draw needn't show every extreme that they name: Every owner holds exactly 6 requests. `node_count`: some request has all 8 nodes live. `cache_len`: some slot uses all 512 positions.
All inputs are finite; a program needn't handle non-finite values.
Results may differ from the reference program's by a relative error of at most 0.01655.
The reference program's roundings to bfloat16 on the way count: a program that leaves them out, or rounds other values in their place, can miss the bound.
Values may be sent and summed in bfloat16 or wider, within the bound.
A program may use at most 256 MiB of HBM per device.

```python
import jax
import jax.numpy as jnp
from jax import lax

FIN = 24576
DF = 8192
QUERY_HEADS = 64
KEY_VALUE_HEADS = 4
HEAD_SIZE = 128
QW = 9216
TREE_SLOTS = 8
REQ_DEV = 6
REQUEST_TOTAL = 24
ROWS = 192
CACHED_POSITIONS = 512


def draw_owner(key, part):
    key = jax.random.fold_in(key, 5)
    shuffled = jax.random.permutation(key, REQUEST_TOTAL)
    return (shuffled // REQ_DEV).astype(jnp.int32)


def draw_node_count(key, part):
    key = jax.random.fold_in(key, 7)
    leading_key, second_key = jax.random.split(key)
    counts = jax.random.randint(leading_key, (REQUEST_TOTAL,), 1, TREE_SLOTS + 1)
    chosen = jax.random.randint(second_key, (), 0, REQUEST_TOTAL)
    return counts.at[chosen].set(TREE_SLOTS).astype(jnp.int32)


def draw_cache_len(key, part):
    key = jax.random.fold_in(key, 9)
    leading_key, second_key = jax.random.split(key)
    lengths = jax.random.randint(leading_key, (REQUEST_TOTAL,), 1, CACHED_POSITIONS + 1)
    chosen = jax.random.randint(second_key, (), 0, REQUEST_TOTAL)
    return lengths.at[chosen].set(CACHED_POSITIONS).astype(jnp.int32)


def draw_owner_draft_cache(key, part):
    key = jax.random.fold_in(key, 11)
    leading_key = jax.random.fold_in(key, 0)
    value_rows = jax.random.normal(leading_key, (REQUEST_TOTAL, CACHED_POSITIONS, 2, KEY_VALUE_HEADS * HEAD_SIZE), jnp.float32)
    return jnp.clip(value_rows, -250.0, 250.0).astype(jnp.bfloat16)


def block_scale(stream_key, dims, pieces, smallest, largest):
    def one(dim, shards_of):
        steps = jax.random.uniform(jax.random.fold_in(jax.random.fold_in(stream_key, 6), dim), (shards_of,), jnp.float32, smallest / len(pieces), largest / len(pieces))
        return jnp.repeat(jnp.exp(steps), dims[dim] // shards_of).reshape((-1,) + (1,) * (len(dims) - dim - 1))

    gain = one(*pieces[0])
    for cut in pieces[1:]:
        gain = gain * one(*cut)
    return gain


def normal_values(own_key, dims, spread, bound, cuts=(), held_as=jnp.bfloat16):
    values = spread * jax.random.normal(own_key, dims, jnp.float32)
    if cuts:
        values = values * block_scale(own_key, dims, cuts, -0.22, 0.18)
    return jnp.clip(values, -bound, bound).astype(held_as)


def setup_inputs(seed: int = 0, part: int = 0) -> dict:
    splits = jax.random.split(jax.random.key(seed), 9)
    part_splits = jax.random.split(jax.random.fold_in(splits[8], part), 9)
    hidden = normal_values(part_splits[0], (ROWS, FIN), 1.0, 6.0, ((0, 4), (1, 4)))
    join_weight = normal_values(splits[1], (FIN, DF), FIN ** -0.5, 0.0390625, ((0, 4), (1, 4)))
    norm_gain = jnp.clip(1.0 + 0.18 * jax.random.normal(splits[2], (DF,), jnp.float32), 0.099609375, 1.8984375).astype(jnp.bfloat16)
    qkv_weight = normal_values(splits[3], (DF, QW), DF ** -0.5, 0.0625, ((0, 16),))
    owner_draft_cache = draw_owner_draft_cache(jax.random.fold_in(jax.random.fold_in(splits[8], part), 71), part)
    node_count = draw_node_count(jax.random.fold_in(jax.random.fold_in(splits[8], part), 71), part)
    owner = draw_owner(jax.random.fold_in(jax.random.fold_in(splits[8], part), 71), part)
    cache_len = draw_cache_len(jax.random.fold_in(jax.random.fold_in(splits[8], part), 71), part)
    return dict(hidden=hidden, join_weight=join_weight, norm_gain=norm_gain, qkv_weight=qkv_weight, owner_draft_cache=owner_draft_cache, node_count=node_count, owner=owner, cache_len=cache_len)


norm_eps = 1e-05

def slot_tables(owner):
    count_all = owner.shape[0]
    same_owner = owner[:, None] == owner[None, :]
    earlier = jnp.arange(count_all)[None, :] < jnp.arange(count_all)[:, None]
    ranking = lax.optimization_barrier(jnp.sum((same_owner & earlier).astype(jnp.int32), axis=1))
    slot_of = (owner * REQ_DEV + ranking).astype(jnp.int32)
    request_of = jnp.zeros((count_all,), jnp.int32).at[slot_of].set(jnp.arange(count_all, dtype=jnp.int32))
    return (slot_of, request_of)

def attend_slot(inputs):
    query_rows, cached_key_rows, cached_value_rows, fresh_key, fresh_value, length, live_nodes = inputs
    scale_factor = HEAD_SIZE ** (-0.5)
    score_cache = jnp.einsum('nkgd,pkd->nkgp', query_rows.astype(jnp.float32), cached_key_rows.astype(jnp.float32)) * scale_factor
    cache_mask = (jnp.arange(CACHED_POSITIONS) < length)[None, None, None, :]
    score_cache = jnp.where(cache_mask, score_cache, -1e+30)
    score_new = jnp.einsum('nkgd,mkd->nkgm', query_rows.astype(jnp.float32), fresh_key.astype(jnp.float32)) * scale_factor
    new_mask = (jnp.arange(TREE_SLOTS)[None, :] <= jnp.arange(TREE_SLOTS)[:, None])[:, None, None, :]
    score_new = jnp.where(new_mask, score_new, -1e+30)
    top_score = jnp.maximum(lax.optimization_barrier(jnp.max(score_cache, axis=-1)), lax.optimization_barrier(jnp.max(score_new, axis=-1)))
    weight_cache = jnp.where(cache_mask, jnp.exp(score_cache - top_score[..., None]), 0.0)
    weight_new = jnp.where(new_mask, jnp.exp(score_new - top_score[..., None]), 0.0)
    denominator = lax.optimization_barrier(jnp.sum(weight_cache, axis=-1)) + lax.optimization_barrier(jnp.sum(weight_new, axis=-1))
    round_cache = lax.optimization_barrier(weight_cache.astype(jnp.bfloat16)).astype(jnp.float32)
    round_new = lax.optimization_barrier(weight_new.astype(jnp.bfloat16)).astype(jnp.float32)
    accum = jnp.einsum('nkgp,pkd->nkgd', round_cache, cached_value_rows.astype(jnp.float32))
    accum = accum + jnp.einsum('nkgm,mkd->nkgd', round_new, fresh_value.astype(jnp.float32))
    result = accum / denominator[..., None]
    alive = (jnp.arange(TREE_SLOTS) < live_nodes)[:, None, None, None]
    result = jnp.where(alive, result, 0.0)
    return result.reshape(TREE_SLOTS, QUERY_HEADS * HEAD_SIZE).astype(jnp.bfloat16)

def reference(hidden, join_weight, norm_gain, qkv_weight, owner_draft_cache, node_count, owner, cache_len):
    joined = jnp.dot(hidden, join_weight, preferred_element_type=jnp.float32).astype(jnp.bfloat16)
    slot_of, request_of = slot_tables(owner)
    joined_slot = joined.reshape(REQUEST_TOTAL, TREE_SLOTS, DF)[request_of].reshape(ROWS, DF)
    widened = joined_slot.astype(jnp.float32)
    mean_sq = lax.optimization_barrier(jnp.mean(widened * widened, axis=1, keepdims=True))
    scaled = (widened * norm_gain.astype(jnp.float32)).astype(jnp.bfloat16)
    query_key_value = jnp.dot(scaled, qkv_weight, preferred_element_type=jnp.float32) * lax.rsqrt(mean_sq + norm_eps)
    query_key_value = query_key_value.astype(jnp.bfloat16)
    query_group_width = QUERY_HEADS // KEY_VALUE_HEADS
    query_rows = query_key_value[:, :QUERY_HEADS * HEAD_SIZE].reshape(REQUEST_TOTAL, TREE_SLOTS, KEY_VALUE_HEADS, query_group_width, HEAD_SIZE)
    fresh_key = query_key_value[:, QUERY_HEADS * HEAD_SIZE:(QUERY_HEADS + KEY_VALUE_HEADS) * HEAD_SIZE].reshape(REQUEST_TOTAL, TREE_SLOTS, KEY_VALUE_HEADS, HEAD_SIZE)
    fresh_value = query_key_value[:, (QUERY_HEADS + KEY_VALUE_HEADS) * HEAD_SIZE:].reshape(REQUEST_TOTAL, TREE_SLOTS, KEY_VALUE_HEADS, HEAD_SIZE)
    live_slot = node_count[request_of]
    cached_key_rows = owner_draft_cache[:, :, 0].reshape(REQUEST_TOTAL, CACHED_POSITIONS, KEY_VALUE_HEADS, HEAD_SIZE)
    cached_value_rows = owner_draft_cache[:, :, 1].reshape(REQUEST_TOTAL, CACHED_POSITIONS, KEY_VALUE_HEADS, HEAD_SIZE)
    return lax.map(attend_slot, (query_rows, cached_key_rows, cached_value_rows, fresh_key, fresh_value, cache_len, live_slot))
```

```python
import jax
import jax.numpy as jnp
from jax import lax
from jax.sharding import PartitionSpec as P

DF = 8192
QUERY_HEADS = 64
KEY_VALUE_HEADS = 4
HEAD_SIZE = 128
TREE_SLOTS = 8
CACHE_BLOCK = 128


norm_eps = 1e-05


def slots(owner, request_per_owner):
    count_all = owner.shape[0]
    same_owner = owner[:, None] == owner[None, :]
    earlier = jnp.arange(count_all)[None, :] < jnp.arange(count_all)[:, None]
    ranking = jnp.sum((same_owner & earlier).astype(jnp.int32), axis=1)
    return owner * request_per_owner + ranking


def body(
    hidden, join_weight, norm_gain, qkv_weight, owner_draft_cache, node_count, owner, cache_len
):
    tensor_count = lax.axis_size("tensor")
    req_here = lax.axis_index("req")
    tensor_here = lax.axis_index("tensor")
    request_per_owner = owner_draft_cache.shape[0]
    count_all = owner.shape[0]
    slot_of = slots(owner, request_per_owner)
    slot_table = slot_of[None, :] == jnp.arange(count_all, dtype=jnp.int32)[:, None]
    rows_all = count_all * TREE_SLOTS
    hidden_all = lax.all_gather(hidden, "req", axis=0, tiled=True)
    partial_sum = jnp.dot(hidden_all, join_weight, preferred_element_type=jnp.float32)
    joined = lax.psum_scatter(partial_sum, "tensor", scatter_dimension=1, tiled=True).astype(
        jnp.bfloat16
    )
    features = joined.shape[1]
    joined = jnp.dot(
        slot_table.astype(jnp.bfloat16),
        joined.reshape(count_all, TREE_SLOTS * features),
        preferred_element_type=jnp.float32,
    ).reshape(rows_all, features)
    scaled = (joined * norm_gain.astype(jnp.float32)).astype(jnp.bfloat16)
    partial_qkv = jnp.dot(scaled, qkv_weight, preferred_element_type=jnp.float32)
    row_squares = jnp.sum(joined * joined, axis=1)
    own_qkv = lax.psum_scatter(partial_qkv, "req", scatter_dimension=0, tiled=True)
    total_squares = lax.dynamic_slice_in_dim(
        lax.psum(row_squares, ("req", "tensor")),
        req_here * request_per_owner * TREE_SLOTS,
        request_per_owner * TREE_SLOTS,
    )
    total_qkv = lax.psum(own_qkv, "tensor")
    query_key_value = (total_qkv * lax.rsqrt(total_squares[:, None] / DF + norm_eps)).astype(
        jnp.bfloat16
    )
    query_group_width = QUERY_HEADS // KEY_VALUE_HEADS
    query_rows = query_key_value[:, : QUERY_HEADS * HEAD_SIZE].reshape(
        request_per_owner, TREE_SLOTS, KEY_VALUE_HEADS, query_group_width, HEAD_SIZE
    )
    fresh_key = query_key_value[
        :, QUERY_HEADS * HEAD_SIZE : (QUERY_HEADS + KEY_VALUE_HEADS) * HEAD_SIZE
    ].reshape(request_per_owner, TREE_SLOTS, KEY_VALUE_HEADS, HEAD_SIZE)
    fresh_value = query_key_value[:, (QUERY_HEADS + KEY_VALUE_HEADS) * HEAD_SIZE :].reshape(
        request_per_owner, TREE_SLOTS, KEY_VALUE_HEADS, HEAD_SIZE
    )
    cached_key_rows = owner_draft_cache[:, :, 0].reshape(
        request_per_owner, CACHE_BLOCK, KEY_VALUE_HEADS, HEAD_SIZE
    )
    cached_value_rows = owner_draft_cache[:, :, 1].reshape(
        request_per_owner, CACHE_BLOCK, KEY_VALUE_HEADS, HEAD_SIZE
    )
    lengths = lax.dynamic_slice_in_dim(cache_len, req_here * request_per_owner, request_per_owner)
    live_all = jnp.sum(jnp.where(slot_table, node_count[None, :], 0), axis=1)
    live_slot = lax.dynamic_slice_in_dim(live_all, req_here * request_per_owner, request_per_owner)
    scale_factor = HEAD_SIZE ** (-0.5)
    positions = tensor_here * CACHE_BLOCK + jnp.arange(CACHE_BLOCK)
    cache_mask = (positions[None, :] < lengths[:, None])[:, None, None, None, :]
    score_cache = (
        jnp.einsum(
            "snkgd,spkd->snkgp", query_rows, cached_key_rows, preferred_element_type=jnp.float32
        )
        * scale_factor
    )
    score_cache = jnp.where(cache_mask, score_cache, -1e30)
    first_block = tensor_here == 0
    new_mask = (jnp.arange(TREE_SLOTS)[None, :] <= jnp.arange(TREE_SLOTS)[:, None]) & first_block
    new_mask = new_mask[None, :, None, None, :]
    score_new = (
        jnp.einsum("snkgd,smkd->snkgm", query_rows, fresh_key, preferred_element_type=jnp.float32)
        * scale_factor
    )
    score_new = jnp.where(new_mask, score_new, -1e30)
    local_top = jnp.maximum(jnp.max(score_cache, axis=-1), jnp.max(score_new, axis=-1))
    top_score = lax.pmax(local_top, "tensor")
    weight_cache = jnp.where(cache_mask, jnp.exp(score_cache - top_score[..., None]), 0.0)
    weight_new = jnp.where(new_mask, jnp.exp(score_new - top_score[..., None]), 0.0)
    denominator = jnp.sum(weight_cache, axis=-1) + jnp.sum(weight_new, axis=-1)
    accum = jnp.einsum(
        "snkgp,spkd->snkgd",
        weight_cache.astype(jnp.bfloat16),
        cached_value_rows,
        preferred_element_type=jnp.float32,
    )
    accum = accum + jnp.einsum(
        "snkgm,smkd->snkgd",
        weight_new.astype(jnp.bfloat16),
        fresh_value,
        preferred_element_type=jnp.float32,
    )
    head_cols = QUERY_HEADS * HEAD_SIZE // tensor_count
    accum_all, denom_all = lax.psum((accum, denominator), "tensor")
    result_all = (accum_all / denom_all[..., None]).reshape(
        request_per_owner, TREE_SLOTS, QUERY_HEADS * HEAD_SIZE
    )
    result = lax.dynamic_slice_in_dim(result_all, tensor_here * head_cols, head_cols, 2)
    alive = (jnp.arange(TREE_SLOTS)[None, :] < live_slot[:, None])[:, :, None]
    return jnp.where(alive, result, 0.0).astype(jnp.bfloat16)


def solution(mesh):
    return jax.shard_map(
        body,
        mesh=mesh,
        in_specs=(
            P(("groups", "req"), "tensor"),
            P("tensor", "req"),
            P(("req", "tensor")),
            P(("req", "tensor"), None),
            P(("groups", "req"), "tensor", None, None),
            P("groups"),
            P("groups"),
            P("groups"),
        ),
        out_specs=P(("groups", "req"), None, "tensor"),
        check_vma=False,
    )
```
